128 devices in a mesh: grid: 16 (over z_lo, y, core), mode: 8 (over z_hi, x).
Axes of the slice: x: 4, y: 4, z: 4 (z_hi: 2, z_lo: 2; z = z_hi * 2 + z_lo), core: 2. Of those that a mesh axis runs over, the one named last changes fastest.
Arguments:
- pod_basis: bfloat16 [524288, 2048], P('grid', 'mode'), may hold values from -0.125 to 0.125
- probe_vectors: float32 [16, 2048], P(None, 'mode'), may hold values from -6 to 6
- drifter_tiles: int32 [16, 4096], P('grid'), may hold values from 0 to 4095, as said below
- tile_counts: int32 [4096], P('grid'), may hold values from 0 to 32, as said below
- stencil_offsets: int32 [4, 16, 4096], P(None, 'grid'), may hold values from 0 to 127
- stencil_weights: float32 [4, 16, 4096], P(None, 'grid'), may hold values from 0.05 to 0.5
- error_scales: float32 [16, 4096], P('grid'), may hold values from 1 to 6
- time_precision: float32 [16, 16], replicated, as said below
Outputs:
- first_product: float32 [16, 2048], P(None, 'mode')
- second_product: float32 [16, 2048], P(None, 'mode')
The draws below stay inside these ranges and needn't reach their ends.
Inputs may be any that keep to these rules, and one draw needn't show every extreme that they name: drifter_tiles[k, j] is a tile of window k, from k * 256 to (k + 1) * 256 - 1; no tile holds more than 32 drifters. tile_counts[t] is the number of entries of drifter_tiles equal to t. `time_precision`: symmetric, every diagonal entry 1, off-diagonal magnitudes of a row sum to less than 1.
All inputs are finite; a program needn't handle non-finite values.
Results may differ from the reference program's by a relative error of at most 0.0029.
The reference program's roundings to bfloat16 on the way (of `probe_bf` and `adjoint`) count: a program that leaves them out, or rounds other values in their place, can miss the bound.
Values may be sent and summed in bfloat16 or wider, within the bound.
A program may use at most 128 MiB of HBM per device.

```python
import math
import jax
import jax.numpy as jnp
from jax import lax

MODES = 2048
NDRIFT = 4096
PROBES = 16
STENCIL = 4
TILE = 128
NWIN = 16
TILES_DEV = 256
NPTS = 524288
NTILES = 4096


tile_capacity = 32


def window_tiles(key):
    slot_total = TILES_DEV * tile_capacity
    key_slots = jax.random.fold_in(key, 1)
    key_order = jax.random.fold_in(key, 2)
    middle = tile_capacity + jax.random.permutation(key_slots, slot_total - tile_capacity - 1)
    chosen = jnp.concatenate([jnp.arange(tile_capacity, dtype=jnp.int32), jnp.full((1,), slot_total - 1, jnp.int32), middle[:NDRIFT - tile_capacity - 1].astype(jnp.int32)])
    shuffled = chosen[jax.random.permutation(key_order, NDRIFT)]
    return (shuffled // tile_capacity).astype(jnp.int32)


def tile_table(key):
    window_keys = jax.vmap(lambda index: jax.random.fold_in(key, index))(jnp.arange(NWIN, dtype=jnp.int32))
    local_tile = jax.vmap(window_tiles)(window_keys)
    window_base = jnp.arange(NWIN, dtype=jnp.int32)[:, None] * TILES_DEV
    return (window_base + local_tile).astype(jnp.int32)


def draw_drifter_tiles(key, part):
    return tile_table(key)


def draw_tile_counts(key, part):
    table = tile_table(key)
    return jnp.zeros((NTILES,), jnp.int32).at[table.reshape(-1)].add(1)


def draw_time_precision(key, part):
    key = jax.random.fold_in(key, 7)
    raw_off = jax.random.uniform(key, (NWIN, NWIN), jnp.float32, -0.5, 0.5)
    sym_off = raw_off + raw_off.T
    eye_mask = jnp.eye(NWIN, dtype=jnp.float32)
    return (sym_off * (1.0 - eye_mask) / NWIN + eye_mask).astype(jnp.float32)


def with_ends(result, stream_key, smallest, largest):
    longest = result.shape.index(max(result.shape))
    spots = []
    for shift in (0, 1):
        where = [jax.random.randint(jax.random.fold_in(stream_key, axis), (), 0, length) for axis, length in enumerate(result.shape)]
        where[longest] = (where[longest] + shift) % result.shape[longest]
        spots.append(tuple(where))
    return result.at[spots[0]].set(smallest).at[spots[1]].set(largest)


def shard_levels(key, dims, cuts, least, largest):
    level, own = 1.0, jax.random.fold_in(key, 6)
    for axis_at, parts in cuts:
        steps = jnp.exp(jax.random.uniform(jax.random.fold_in(own, axis_at), (parts,), jnp.float32, least / len(cuts), largest / len(cuts)))
        level = level * jnp.repeat(steps, dims[axis_at] // parts).reshape([-1 if axis == axis_at else 1 for axis in range(len(dims))])
    return level


def gaussian(stream_key, extent, width, most, pieces=(), kind=jnp.bfloat16):
    factor_of = shard_levels(stream_key, extent, pieces, -0.22, 0.18) if pieces else 1.0
    entries = jax.random.normal(stream_key, extent, jnp.float32) * width * factor_of
    return jnp.minimum(jnp.maximum(entries, -most), most).astype(kind)


def setup_inputs(seed: int = 0) -> dict:
    key_list = jax.random.split(jax.random.key(seed), 9)
    return {
        "pod_basis": gaussian(key_list[0], (NPTS, MODES), MODES ** -0.5, 0.125, ((0, 16), (1, 8))),
        "probe_vectors": gaussian(key_list[1], (PROBES, MODES), 1.0, 6.0, ((1, 8),), jnp.float32),
        "drifter_tiles": draw_drifter_tiles(jax.random.fold_in(key_list[8], 71), 0),
        "tile_counts": draw_tile_counts(jax.random.fold_in(key_list[8], 71), 0),
        "stencil_offsets": with_ends(jax.random.randint(key_list[4], (STENCIL, NWIN, NDRIFT), 0, TILE), jax.random.fold_in(key_list[4], 1), 0, TILE - 1).astype(jnp.int32),
        "stencil_weights": jnp.clip(0.05 + 0.45 * jax.random.uniform(key_list[5], (STENCIL, NWIN, NDRIFT), jnp.float32) ** shard_levels(key_list[5], (STENCIL, NWIN, NDRIFT), ((1, 16),), -0.2, 0.2), 0.05, 0.5),
        "error_scales": jnp.clip(jnp.exp(math.log(6.0) - 1.7917595 * jax.random.uniform(key_list[6], (NWIN, NDRIFT), jnp.float32) ** shard_levels(key_list[6], (NWIN, NDRIFT), ((0, 16),), -0.2, 0.2)), 1.0, 6.0),
        "time_precision": draw_time_precision(jax.random.fold_in(key_list[8], 71), 0),
    }


def hessian(vector, pod_basis, point_rows, stencil_weights, obs_gain, time_precision):
    probe_bf = vector.astype(jnp.bfloat16)
    state_rows = jnp.dot(probe_bf, pod_basis.T, preferred_element_type=jnp.float32)
    picked = state_rows[:, point_rows]
    scaled = obs_gain[None] * lax.optimization_barrier(jnp.sum(stencil_weights[None] * picked, axis=1))
    coupled = jnp.einsum('kl,pld->pkd', time_precision, scaled, precision=lax.Precision.HIGHEST)
    weighted = obs_gain[None] * coupled
    spread = (stencil_weights[None] * weighted[:, None]).reshape(PROBES, -1)
    adjoint = jnp.zeros((PROBES, NPTS), jnp.float32).at[:, point_rows.reshape(-1)].add(spread)
    adjoint_bf = adjoint.astype(jnp.bfloat16)
    increment = jnp.dot(adjoint_bf, pod_basis, preferred_element_type=jnp.float32)
    return vector + increment

def reference(pod_basis, probe_vectors, drifter_tiles, tile_counts, stencil_offsets, stencil_weights, error_scales, time_precision):
    point_rows = (drifter_tiles[None] * TILE + stencil_offsets).astype(jnp.int32)
    obs_gain = error_scales / jnp.sqrt(tile_counts[drifter_tiles].astype(jnp.float32))
    first_product = hessian(probe_vectors, pod_basis, point_rows, stencil_weights, obs_gain, time_precision)
    second_product = hessian(first_product, pod_basis, point_rows, stencil_weights, obs_gain, time_precision)
    return (first_product, second_product)
```

```python
import functools

import jax
import jax.numpy as jnp
from jax import lax
from jax.experimental import pallas as pl
from jax.experimental.pallas import tpu as pltpu
from jax.sharding import PartitionSpec as P

F32 = jnp.float32
BF16 = jnp.bfloat16
I32 = jnp.int32
MESH = pl.DeviceIdType.MESH

LOADS = 16
PARTS = 4
PART_H = 16

NN = (((1,), (0,)), ((), ()))
NT = (((1,), (1,)), ((), ()))


def mm(a, b, dims):
    return lax.dot_general(a, b, dims, preferred_element_type=F32)


def lanes_of(x, idx):
    return jnp.take_along_axis(x, idx, axis=1, mode="promise_in_bounds")


def kernel(
    n_grid,
    n_mode,
    basis,
    probe,
    tiles,
    counts,
    offs,
    wts,
    scales,
    prec,
    out1,
    out2,
    B,
    WT,
    offS,
    wS,
    jrowS,
    jlaneS,
    hiJ,
    loJ,
    gainJ,
    packJ,
    partial,
    rs_in,
    X,
    Z,
    R,
    C,
    D,
    S,
    Fw,
    acc_out,
    ar_in,
    vec,
    load_sem,
    rs_send,
    rs_recv,
    a1_send,
    a1_recv,
    a2_send,
    a2_recv,
    ag_send,
    ag_recv,
    ar_send,
    ar_recv,
):
    g = lax.axis_index("grid")
    m = lax.axis_index("mode")
    rows = basis.shape[0] // LOADS

    def load(i):
        return pltpu.make_async_copy(
            basis.at[pl.ds(i * rows, rows)], B.at[pl.ds(i * rows, rows)], load_sem.at[i]
        )

    for i in range(LOADS):
        load(i).start()

    barrier = pltpu.get_barrier_semaphore()
    for d in range(1, n_mode):
        pl.semaphore_signal(
            barrier, inc=1, device_id=(g, lax.rem(m + d, n_mode)), device_id_type=MESH
        )
    for d in range(1, n_grid):
        pl.semaphore_signal(
            barrier, inc=1, device_id=(lax.rem(g + d, n_grid), m), device_id_type=MESH
        )

    sub = lax.broadcasted_iota(I32, (256, 256), 0)
    lan = lax.broadcasted_iota(I32, (256, 256), 1)
    upto = (sub <= lan).astype(BF16)
    ones = jnp.ones((16, 256), BF16)
    base = jnp.zeros((16, 256), F32)
    first = lax.broadcasted_iota(I32, (16, 256), 0) == 0
    count_row = jnp.broadcast_to(counts[...].astype(F32), (16, 256))
    inverse = jnp.zeros((64, 256), F32)
    hsub = lax.broadcasted_iota(I32, (64, 256), 0)
    lsub = lax.broadcasted_iota(I32, (128, 256), 0)
    jlan = lax.broadcasted_iota(I32, (1, 256), 1)
    for b in range(16):
        cols = pl.ds(b * 256, 256)
        lt = tiles[0:1, cols] - g * 256
        onehot = (sub == lt).astype(F32)
        onehot_bf = onehot.astype(BF16)
        within = mm(onehot_bf, upto, NN)
        looked = mm(jnp.where(first, base, count_row).astype(BF16), onehot_bf, NN)
        rank = jnp.sum(onehot * within, axis=0, keepdims=True) + looked[0:1] - 1.0
        base = base + mm(ones, onehot_bf, NT)
        gain = scales[0:1, cols] / jnp.sqrt(looked[1:2])
        hi = lt >> 2
        lo = (lt & 3) * 32 + rank.astype(I32)
        packed = offs[0, 0:1, cols]
        for s in range(1, 4):
            packed = packed | (offs[s, 0:1, cols] << (7 * s))
        for r in range(2):
            row = pl.ds(2 * b + r, 1)
            hiJ[row, :] = hi[:, 128 * r : 128 * r + 128]
            loJ[row, :] = lo[:, 128 * r : 128 * r + 128]
            gainJ[row, :] = gain[:, 128 * r : 128 * r + 128]
            packJ[row, :] = packed[:, 128 * r : 128 * r + 128]
        j = jlan + b * 256
        low = lsub == lo
        jrow1 = jnp.where(low, ((j >> 7) + 1).astype(F32), 0.0).astype(BF16)
        jlane = jnp.where(low, (j & 127).astype(F32), 0.0).astype(BF16)
        high = (hsub == hi).astype(F32).astype(BF16)
        inverse = inverse + mm(high, jnp.concatenate([jrow1, jlane], axis=0), NT)
    jrowS[...] = inverse[:, :128].astype(I32) - 1
    jlaneS[...] = inverse[:, 128:].astype(I32)

    for half in range(2):
        at = [32 * half + 8 * i for i in range(4)]
        want = [jrowS[a : a + 8, :] for a in at]
        lane = [jlaneS[a : a + 8, :] for a in at]

        def place(r, got):
            src = [packJ[pl.ds(r, 1), :]]
            src += [wts[s, 0:1, pl.ds(pl.multiple_of(r * 128, 128), 128)] for s in range(4)]
            src = [jnp.broadcast_to(x, (8, 128)) for x in src]
            new = []
            for i in range(4):
                here = want[i] == r
                for k in range(5):
                    new.append(jnp.where(here, lanes_of(src[k], lane[i]), got[5 * i + k]))
            return tuple(new)

        zero = [jnp.zeros((8, 128), I32)] + [jnp.zeros((8, 128), F32)] * 4
        got = lax.fori_loop(0, 32, place, tuple(zero * 4), unroll=2)
        for i in range(4):
            for s in range(4):
                offS[s, pl.ds(at[i], 8), :] = (got[5 * i] >> (7 * s)) & 127
                wS[s, pl.ds(at[i], 8), :] = got[5 * i + 1 + s]

    def stencil_matrix(h, carry):
        point = lax.broadcasted_iota(I32, (128, 128), 0)
        w = jnp.zeros((128, 128), F32)
        for s in range(4):
            w = w + jnp.where(point == offS[s, pl.ds(h, 1), :], wS[s, pl.ds(h, 1), :], 0.0)
        w_hi = w.astype(BF16)
        w_lo = (w - w_hi.astype(F32)).astype(BF16)
        at = pl.multiple_of(h * 128, 128)
        WT[pl.ds(at, 128), 0:128] = w_hi
        WT[pl.ds(at, 128), 128:256] = w_lo
        return carry

    vec[...] = probe[...]
    lane_group = lax.broadcasted_iota(I32, (8, 128), 1) >> 5
    group16 = lax.broadcasted_iota(I32, (16, 128), 1) >> 5

    def hessian(t, out):
        v_bf = vec[...].astype(BF16)

        def state(h):
            at = pl.multiple_of(h * 512, 512)
            return mm(v_bf, B[pl.ds(at, 512), :], NT)

        def observe(st, h, c):
            for half in range(2):
                acc = None
                for s in range(4):
                    idx = jnp.broadcast_to(offS[s, pl.ds(h, 1), :], (8, 128))
                    w = wS[s, pl.ds(h, 1), :]
                    val = None
                    for q in range(4):
                        one = lanes_of(st[8 * half : 8 * half + 8, 128 * q : 128 * q + 128], idx)
                        val = one if q == 0 else jnp.where(lane_group == q, one, val)
                    acc = val * w if s == 0 else acc + val * w
                at = c * 256 + half * 128 + (h - c * PART_H)
                partial[t, pl.ds(at, 8, stride=16), :] = acc

        def rs_copy(c, d):
            peer = lax.rem(m + d, n_mode)
            return pltpu.make_async_remote_copy(
                src_ref=partial.at[t, pl.ds(c * 256 + 32 * peer, 32)],
                dst_ref=rs_in.at[t, pl.ds(c * 224 + 32 * (d - 1), 32)],
                send_sem=rs_send.at[t, c],
                recv_sem=rs_recv.at[t, c],
                device_id=(g, peer),
                device_id_type=MESH,
            )

        for c in range(PARTS):
            if t == 0:
                for i in range(LOADS // PARTS):
                    load(c * (LOADS // PARTS) + i).wait()

            def step(i, st):
                h = c * PART_H + i
                nxt = state(h + 1)
                observe(st, h, c)
                return nxt

            st = lax.fori_loop(0, PART_H - 1, step, state(c * PART_H), unroll=3)
            observe(st, c * PART_H + PART_H - 1, c)
            if t == 0 and c == 0:
                pl.semaphore_wait(barrier, n_mode + n_grid - 2)
            for d in range(1, n_mode):
                rs_copy(c, d).start()

        if t == 0:
            lax.fori_loop(0, 64, stencil_matrix, 0, unroll=2)

        hi = [hiJ[8 * i : 8 * i + 8, :] for i in range(4)]
        lo = [loJ[8 * i : 8 * i + 8, :] for i in range(4)]
        got = tuple([jnp.zeros((8, 128), F32)] * 8)
        for c in range(PARTS):
            whole = rs_in.at[t, pl.ds(c * 224, 224)]
            pltpu.make_async_copy(whole, whole, rs_recv.at[t, c]).wait()
            total = partial[t, pl.ds(pl.multiple_of(c * 256 + 32 * m, 32), 32), :]
            for d in range(n_mode - 1):
                total = total + rs_in[t, pl.ds(c * 224 + 32 * d, 32), :]
            X[pl.ds(c * 32, 32), :] = total

            def to_drifters(i, got):
                h = c * PART_H + i
                new = list(got)
                here = [hi[k] == h for k in range(4)]
                for p in range(2):
                    row = jnp.broadcast_to(X[pl.ds(c * 32 + 16 * p + i, 1), :], (8, 128))
                    for k in range(4):
                        new[4 * p + k] = jnp.where(here[k], lanes_of(row, lo[k]), got[4 * p + k])
                return tuple(new)

            got = lax.fori_loop(0, PART_H, to_drifters, got, unroll=4)
        for p in range(2):
            for k in range(4):
                val = got[4 * p + k] * gainJ[8 * k : 8 * k + 8, :]
                for q in range(4):
                    Z[t, 4 * k + q, 2 * p : 2 * p + 2, :] = val[2 * q : 2 * q + 2]

        def grid_copy(d, src, dst, send, recv):
            peer = lax.rem(g + d, n_grid)
            return pltpu.make_async_remote_copy(
                src_ref=src.at[t, peer],
                dst_ref=dst.at[t, g],
                send_sem=send.at[t],
                recv_sem=recv.at[t],
                device_id=(peer, m),
                device_id_type=MESH,
            )

        def wait_bytes(ref, sem):
            pltpu.make_async_copy(ref, ref, sem).wait()

        for d in range(1, n_grid):
            grid_copy(d, Z, R, a1_send, a1_recv).start()
        R[t, g] = Z[t, g]
        wait_bytes(R.at[t, pl.ds(0, n_grid - 1)], a1_recv.at[t])
        obs = [R[t, l] for l in range(16)]
        for k in range(16):
            acc = prec[k, 0] * obs[0]
            for l in range(1, 16):
                acc = acc + prec[k, l] * obs[l]
            C[t, k] = acc
        for d in range(1, n_grid):
            grid_copy(d, C, D, a2_send, a2_recv).start()
        D[t, g] = C[t, g]
        wait_bytes(D.at[t, pl.ds(0, n_grid - 1)], a2_recv.at[t])

        want = [jrowS[8 * i : 8 * i + 8, :] for i in range(8)]
        lane = [jlaneS[8 * i : 8 * i + 8, :] for i in range(8)]

        def to_slots(i, got):
            new = list(got)
            for r in range(2):
                jr = 2 * i + r
                here = [want[k] == jr for k in range(8)]
                gain = gainJ[pl.ds(jr, 1), :]
                for p in range(2):
                    row = D[t, i, 2 * p + r : 2 * p + r + 1, :] * gain
                    row = jnp.broadcast_to(row, (8, 128))
                    for k in range(8):
                        new[8 * p + k] = jnp.where(
                            here[k], lanes_of(row, lane[k]), new[8 * p + k]
                        )
            return tuple(new)

        got = lax.fori_loop(0, 16, to_slots, tuple([jnp.zeros((8, 128), F32)] * 16), unroll=2)
        for p in range(2):
            for k in range(8):
                S[t, pl.ds((k // 2) * 32 + 16 * p + 8 * (k % 2), 8), :] = got[8 * p + k]

        def ag_copy(c, d):
            return pltpu.make_async_remote_copy(
                src_ref=S.at[t, pl.ds(c * 32, 32)],
                dst_ref=Fw.at[t, pl.ds(c * 256 + 32 * m, 32)],
                send_sem=ag_send.at[t, c],
                recv_sem=ag_recv.at[t, c],
                device_id=(g, lax.rem(m + d, n_mode)),
                device_id_type=MESH,
            )

        for c in range(PARTS):
            for d in range(1, n_mode):
                ag_copy(c, d).start()
        for c in range(PARTS):
            own = pl.ds(pl.multiple_of(c * 256 + 32 * m, 32), 32)
            Fw[t, own, :] = S[t, pl.ds(c * 32, 32), :]

        def spread(h, c):
            lhs = []
            for half in range(2):
                at = c * 256 + half * 128 + (h - c * PART_H)
                lhs.append(Fw[t, pl.ds(at, 8, stride=16), :])
            val = jnp.concatenate(lhs, axis=0)
            v_hi = val.astype(BF16).astype(F32)
            v_lo = val - v_hi
            his = [jnp.where(group16 == q, v_hi, 0.0) for q in range(4)]
            los = [jnp.where(group16 == q, v_lo, 0.0) for q in range(4)]
            his = jnp.concatenate(his, axis=0).astype(BF16)
            los = jnp.concatenate(los, axis=0).astype(BF16)
            at = pl.multiple_of(h * 128, 128)
            mat = WT[pl.ds(at, 128), :]
            both = jnp.concatenate([his, his], axis=1)
            adj = mm(both, mat, NT) + mm(los, mat[:, :128], NT)
            adj = jnp.concatenate([adj[16 * q : 16 * q + 16] for q in range(4)], axis=1)
            return adj.astype(BF16)

        def project(adj, h):
            at = pl.multiple_of(h * 512, 512)
            return mm(adj, B[pl.ds(at, 512), :], NN)

        acc = jnp.zeros((16, 256), F32)
        for c in range(PARTS):
            wait_bytes(Fw.at[t, pl.ds(c * 256, 224)], ag_recv.at[t, c])

            def back(i, carry):
                acc, adj = carry
                h = c * PART_H + i
                nxt = spread(h + 1, c)
                return acc + project(adj, h), nxt

            acc, adj = lax.fori_loop(
                0, PART_H - 1, back, (acc, spread(c * PART_H, c)), unroll=3
            )
            acc = acc + project(adj, c * PART_H + PART_H - 1)
        acc_out[t] = acc

        for d in range(1, n_grid):
            peer = lax.rem(g + d, n_grid)
            pltpu.make_async_remote_copy(
                src_ref=acc_out.at[t],
                dst_ref=ar_in.at[t, g],
                send_sem=ar_send.at[t],
                recv_sem=ar_recv.at[t],
                device_id=(peer, m),
                device_id_type=MESH,
            ).start()
        ar_in[t, g] = acc
        wait_bytes(ar_in.at[t, pl.ds(0, n_grid - 1)], ar_recv.at[t])
        total = ar_in[t, 0]
        for l in range(1, n_grid):
            total = total + ar_in[t, l]
        total = vec[...] + total
        vec[...] = total
        out[...] = total

    hessian(0, out1)
    hessian(1, out2)

    for t in range(2):
        for c in range(PARTS):
            for sem in (rs_send, ag_send):
                piece = rs_in.at[t, pl.ds(c * 224, 224)]
                pltpu.make_async_copy(piece, piece, sem.at[t, c]).wait()
        for ref, sem in ((R, a1_send), (D, a2_send), (ar_in, ar_send)):
            piece = ref.at[t, pl.ds(0, n_grid - 1)]
            pltpu.make_async_copy(piece, piece, sem.at[t]).wait()


def local(
    pod_basis,
    probe_vectors,
    drifter_tiles,
    tile_counts,
    stencil_offsets,
    stencil_weights,
    error_scales,
    time_precision,
    *,
    n_grid,
    n_mode,
):
    vmem = pl.BlockSpec(memory_space=pltpu.VMEM)
    dma = pltpu.SemaphoreType.DMA
    table = pltpu.VMEM((64, 128), I32)
    drift_f = pltpu.VMEM((32, 128), F32)
    drift_i = pltpu.VMEM((32, 128), I32)
    return pl.pallas_call(
        functools.partial(kernel, n_grid, n_mode),
        out_shape=(jax.ShapeDtypeStruct(probe_vectors.shape, F32),) * 2,
        in_specs=[
            pl.BlockSpec(memory_space=pl.ANY),
            vmem,
            vmem,
            vmem,
            vmem,
            vmem,
            vmem,
            pl.BlockSpec(memory_space=pltpu.SMEM),
        ],
        out_specs=(vmem, vmem),
        scratch_shapes=[
            pltpu.VMEM(pod_basis.shape, BF16),
            pltpu.VMEM((64 * 128, 256), BF16),
            pltpu.VMEM((4, 64, 128), I32),
            pltpu.VMEM((4, 64, 128), F32),
            table,
            table,
            drift_i,
            drift_i,
            drift_f,
            drift_i,
            pltpu.VMEM((2, 1024, 128), F32),
            pltpu.VMEM((2, 896, 128), F32),
            pltpu.VMEM((128, 128), F32),
            pltpu.VMEM((2, 16, 4, 128), F32),
            pltpu.VMEM((2, 16, 4, 128), F32),
            pltpu.VMEM((2, 16, 4, 128), F32),
            pltpu.VMEM((2, 16, 4, 128), F32),
            pltpu.VMEM((2, 128, 128), F32),
            pltpu.VMEM((2, 1024, 128), F32),
            pltpu.VMEM((2, 16, 256), F32),
            pltpu.VMEM((2, 16, 16, 256), F32),
            pltpu.VMEM((16, 256), F32),
            dma((LOADS,)),
            dma((2, PARTS)),
            dma((2, PARTS)),
            dma((2,)),
            dma((2,)),
            dma((2,)),
            dma((2,)),
            dma((2, PARTS)),
            dma((2, PARTS)),
            dma((2,)),
            dma((2,)),
        ],
        compiler_params=pltpu.CompilerParams(
            collective_id=0, has_side_effects=True, vmem_limit_bytes=40 * 1024 * 1024
        ),
    )(
        pod_basis,
        probe_vectors,
        drifter_tiles,
        tile_counts.reshape(1, -1),
        stencil_offsets,
        stencil_weights,
        error_scales,
        time_precision,
    )


def solution(mesh):
    return jax.shard_map(
        functools.partial(local, n_grid=mesh.shape["grid"], n_mode=mesh.shape["mode"]),
        mesh=mesh,
        in_specs=(
            P("grid", "mode"),
            P(None, "mode"),
            P("grid", None),
            P("grid"),
            P(None, "grid", None),
            P(None, "grid", None),
            P("grid", None),
            P(),
        ),
        out_specs=(P(None, "mode"), P(None, "mode")),
        check_vma=False,
    )
```

```python
import functools

import jax
import jax.numpy as jnp
from jax import lax
from jax.experimental import pallas as pl
from jax.experimental.pallas import tpu as pltpu
from jax.sharding import PartitionSpec as P

F32 = jnp.float32
BF16 = jnp.bfloat16
I32 = jnp.int32
MESH = pl.DeviceIdType.MESH

LOADS = 16
GROUP = 4

NN = (((1,), (0,)), ((), ()))
NT = (((1,), (1,)), ((), ()))


def mm(a, b, dims):
    return lax.dot_general(a, b, dims, preferred_element_type=F32)


def lanes_of(x, idx):
    return jnp.take_along_axis(x, idx, axis=1, mode="promise_in_bounds")


def split(x):
    hi = x.astype(BF16)
    return hi, (x - hi.astype(F32)).astype(BF16)


def kernel(
    n_grid,
    n_mode,
    basis,
    probe_hbm,
    tiles_hbm,
    counts_hbm,
    offs_hbm,
    wts_hbm,
    scales_hbm,
    prec_hbm,
    out1,
    out2,
    B,
    WT,
    tiles,
    counts,
    offs,
    wts,
    scales,
    prec,
    offS,
    wS,
    jrowS,
    jlaneS,
    hiJ,
    gainJ,
    packJ,
    lowJ,
    partial,
    parts,
    Z,
    R,
    C,
    D,
    Y,
    acc_out,
    ar_in,
    vec,
    load_sem,
    small_sem,
    e1_send,
    e1_recv,
    e2_send,
    e2_recv,
    ar_send,
    ar_recv,
):
    g = lax.axis_index("grid")
    m = lax.axis_index("mode")
    n_all = n_grid * n_mode
    me = g * n_mode + m
    rows = basis.shape[0] // LOADS

    small = [
        pltpu.make_async_copy(src, dst, small_sem.at[i])
        for i, (src, dst) in enumerate(
            (
                (tiles_hbm, tiles),
                (counts_hbm, counts),
                (offs_hbm, offs),
                (scales_hbm, scales),
                (wts_hbm, wts),
                (probe_hbm, vec),
                (prec_hbm, prec),
            )
        )
    ]
    for copy in small:
        copy.start()

    def load(i):
        return pltpu.make_async_copy(
            basis.at[pl.ds(i * rows, rows)], B.at[pl.ds(i * rows, rows)], load_sem.at[i]
        )

    for i in range(LOADS):
        load(i).start()

    def window_at(i):
        far = i // 4
        dy = jnp.where(far == 0, 2, jnp.where(far == 1, 1, jnp.where(far == 2, 3, 0)))
        dz = 1 - (i // 2) % 2
        dc = 1 - i % 2
        z = (g // 8 + dz) % 2
        y = ((g // 2) % 4 + dy) % 4
        return z * 8 + y * 2 + (g + dc) % 2

    def mode_at(dx, dz):
        return ((m // 4 + dz) % 2) * 4 + (m % 4 + dx) % 4

    modes = [mode_at(dx, dz) for dx, dz in ((2, 1), (1, 1), (3, 1), (0, 1), (2, 0), (1, 0), (3, 0))]

    barrier = pltpu.get_barrier_semaphore()

    def greet(i):
        there = window_at(i)
        for peer in modes + ([m] if i < n_grid - 1 else []):
            pl.semaphore_signal(barrier, inc=1, device_id=(there, peer), device_id_type=MESH)

    for copy in small:
        copy.wait()
    sub = lax.broadcasted_iota(I32, (256, 256), 0)
    lan = lax.broadcasted_iota(I32, (256, 256), 1)
    upto = (sub <= lan).astype(BF16)
    ones = jnp.ones((16, 256), BF16)
    base = jnp.zeros((16, 256), F32)
    first = lax.broadcasted_iota(I32, (16, 256), 0) == 0
    count_row = jnp.broadcast_to(counts[...].astype(F32), (16, 256))
    inverse = jnp.zeros((64, 256), F32)
    hsub = lax.broadcasted_iota(I32, (64, 256), 0)
    lsub = lax.broadcasted_iota(I32, (128, 256), 0)
    jlan = lax.broadcasted_iota(I32, (1, 256), 1)
    for b in range(16):
        greet(b)
        cols = pl.ds(b * 256, 256)
        lt = tiles[0:1, cols] - g * 256
        onehot = (sub == lt).astype(F32)
        onehot_bf = onehot.astype(BF16)
        within = mm(onehot_bf, upto, NN)
        looked = mm(jnp.where(first, base, count_row).astype(BF16), onehot_bf, NN)
        rank = jnp.sum(onehot * within, axis=0, keepdims=True) + looked[0:1] - 1.0
        base = base + mm(ones, onehot_bf, NT)
        hi = lt >> 2
        lo = (lt & 3) * 32 + rank.astype(I32)
        hiJ[0:1, cols] = hi
        gainJ[0:1, cols] = scales[0:1, cols] / jnp.sqrt(looked[1:2])
        packed = offs[0, 0:1, cols]
        for s in range(1, 4):
            packed = packed | (offs[s, 0:1, cols] << (7 * s))
        packJ[0:1, cols] = packed
        j = jlan + b * 256
        low = lsub == lo
        lowJ[:, cols] = low.astype(F32).astype(BF16)
        jrow1 = jnp.where(low, ((j >> 7) + 1).astype(F32), 0.0).astype(BF16)
        jlane = jnp.where(low, (j & 127).astype(F32), 0.0).astype(BF16)
        high = (hsub == hi).astype(F32).astype(BF16)
        inverse = inverse + mm(high, jnp.concatenate([jrow1, jlane], axis=0), NT)
    jrowS[...] = inverse[:, :128].astype(I32) - 1
    jlaneS[...] = inverse[:, 128:].astype(I32)

    for half in range(2):
        at = [32 * half + 8 * i for i in range(4)]
        want = [jrowS[a : a + 8, :] for a in at]
        lane = [jlaneS[a : a + 8, :] for a in at]

        def place(r, got):
            cols = pl.ds(pl.multiple_of(r * 128, 128), 128)
            src = [packJ[0:1, cols]] + [wts[s, 0:1, cols] for s in range(4)]
            src = [jnp.broadcast_to(x, (8, 128)) for x in src]
            new = []
            for i in range(4):
                here = want[i] == r
                for k in range(5):
                    new.append(jnp.where(here, lanes_of(src[k], lane[i]), got[5 * i + k]))
            return tuple(new)

        zero = [jnp.zeros((8, 128), I32)] + [jnp.zeros((8, 128), F32)] * 4
        got = lax.fori_loop(0, 32, place, tuple(zero * 4), unroll=2)
        for i in range(4):
            for s in range(4):
                offS[s, pl.ds(at[i], 8), :] = (got[5 * i] >> (7 * s)) & 127
                wS[s, pl.ds(at[i], 8), :] = got[5 * i + 1 + s]

    def stencil_matrix(h, carry):
        point = lax.broadcasted_iota(I32, (128, 128), 0)
        w = jnp.zeros((128, 128), F32)
        for s in range(4):
            w = w + jnp.where(point == offS[s, pl.ds(h, 1), :], wS[s, pl.ds(h, 1), :], 0.0)
        w_hi, w_lo = split(w)
        at = pl.multiple_of(h * 128, 128)
        WT[pl.ds(at, 128), 0:128] = w_hi
        WT[pl.ds(at, 128), 128:256] = w_lo
        return carry

    lane_group = lax.broadcasted_iota(I32, (8, 128), 1) >> 5
    group16 = lax.broadcasted_iota(I32, (16, 128), 1) >> 5

    def wait_bytes(ref, sem):
        pltpu.make_async_copy(ref, ref, sem).wait()

    def hessian(t, out):
        v_bf = vec[...].astype(BF16)

        def state(n):
            at = pl.multiple_of(n * GROUP * 512, GROUP * 512)
            return mm(v_bf, B[pl.ds(at, GROUP * 512), :], NT)

        def observe(st, n):
            for k in range(GROUP):
                h = n * GROUP + k
                for half in range(2):
                    acc = None
                    for s in range(4):
                        idx = jnp.broadcast_to(offS[s, pl.ds(h, 1), :], (8, 128))
                        w = wS[s, pl.ds(h, 1), :]
                        val = None
                        for q in range(4):
                            at = 512 * k + 128 * q
                            one = lanes_of(st[8 * half : 8 * half + 8, at : at + 128], idx)
                            val = one if q == 0 else jnp.where(lane_group == q, one, val)
                        acc = val * w if s == 0 else acc + val * w
                    at = (h // 16) * 256 + half * 128 + h % 16
                    partial[pl.ds(at, 8, stride=16), :] = acc

        def step(n, st):
            if t == 0:
                load(n + 1).wait()
            nxt = state(n + 1)
            observe(st, n)
            return nxt

        if t == 0:
            load(0).wait()
        st = lax.fori_loop(0, LOADS - 1, step, state(0))
        observe(st, LOADS - 1)

        p_hi, p_lo = split(partial[...])
        parts[:, 0:128] = p_hi
        parts[:, 128:256] = p_lo
        if t == 0:
            pl.semaphore_wait(barrier, n_all - 1)

        def send_piece(there, peer):
            at = there * n_mode + peer
            pltpu.make_async_remote_copy(
                src_ref=Z.at[t, at],
                dst_ref=R.at[t, me],
                send_sem=e1_send.at[t],
                recv_sem=e1_recv.at[t],
                device_id=(there, peer),
                device_id_type=MESH,
            ).start()

        def to_drifters(i, carry):
            there = window_at(i)
            cols = pl.ds(pl.multiple_of(there * 256, 256), 256)
            low = lowJ[:, cols]
            picked = mm(parts[...], jnp.concatenate([low, low], axis=0), NN)
            mask = (lax.broadcasted_iota(I32, (64, 256), 0) == hiJ[0:1, cols]).astype(F32)
            picked = picked.reshape(4, 16, 16, 256) * mask.reshape(4, 1, 16, 256)
            val = jnp.sum(jnp.sum(picked, axis=0), axis=1)
            val = val * gainJ[0:1, cols]
            for k in range(n_mode):
                for r in range(2):
                    Z[t, there * n_mode + k, 2 * r : 2 * r + 2, :] = val[
                        2 * k : 2 * k + 2, 128 * r : 128 * r + 128
                    ]
            for peer in modes:
                send_piece(there, peer)

            @pl.when(i < n_grid - 1)
            def _():
                send_piece(there, m)

            return carry

        lax.fori_loop(0, n_grid, to_drifters, 0)
        R[t, me] = Z[t, me]

        if t == 0:
            lax.fori_loop(0, 64, stencil_matrix, 0, unroll=2)

        wait_bytes(R.at[t, pl.ds(0, n_all - 1)], e1_recv.at[t])
        obs = []
        for l in range(16):
            total = R[t, l * n_mode]
            for k in range(1, n_mode):
                total = total + R[t, l * n_mode + k]
            obs.append(total)

        def couple(i, carry):
            there = window_at(i)
            terms = [prec[there, l] * obs[l] for l in range(16)]
            while len(terms) > 1:
                terms = [a + b for a, b in zip(terms[::2], terms[1::2])]
            C[t, there] = terms[0]

            def send_back(peer):
                pltpu.make_async_remote_copy(
                    src_ref=C.at[t, there],
                    dst_ref=D.at[t, me],
                    send_sem=e2_send.at[t],
                    recv_sem=e2_recv.at[t],
                    device_id=(there, peer),
                    device_id_type=MESH,
                ).start()

            for peer in modes:
                send_back(peer)

            @pl.when(i < n_grid - 1)
            def _():
                send_back(m)

            return carry

        lax.fori_loop(0, n_grid, couple, 0)
        D[t, me] = C[t, g]
        wait_bytes(D.at[t, pl.ds(0, n_all - 1)], e2_recv.at[t])

        def gather_rows(i, carry):
            for r in range(2):
                cols = pl.ds(pl.multiple_of((2 * i + r) * 128, 128), 128)
                gain = gainJ[0:1, cols]
                for k in range(n_mode):
                    val = D[t, i * n_mode + k, 2 * r : 2 * r + 2, :]
                    Y[pl.ds(i * 32 + 16 * r + 2 * k, 2), :] = val * gain
            return carry

        lax.fori_loop(0, n_grid, gather_rows, 0, unroll=2)

        def slots(h):
            row = jnp.broadcast_to(jrowS[pl.ds(h, 1), :], (8, 128))
            idx = jnp.broadcast_to(jlaneS[pl.ds(h, 1), :], (8, 128))
            got = [jnp.zeros((8, 128), F32)] * 2
            for jr in range(32):
                here = row == jr
                for half in range(2):
                    src = Y[16 * jr + 8 * half : 16 * jr + 8 * half + 8, :]
                    got[half] = jnp.where(here, lanes_of(src, idx), got[half])
            return jnp.concatenate(got, axis=0)

        def spread(val, h):
            v_hi = val.astype(BF16).astype(F32)
            v_lo = val - v_hi
            his = [jnp.where(group16 == q, v_hi, 0.0) for q in range(4)]
            los = [jnp.where(group16 == q, v_lo, 0.0) for q in range(4)]
            his = jnp.concatenate(his, axis=0).astype(BF16)
            los = jnp.concatenate(los, axis=0).astype(BF16)
            at = pl.multiple_of(h * 128, 128)
            mat = WT[pl.ds(at, 128), :]
            both = jnp.concatenate([his, his], axis=1)
            los = jnp.concatenate([los, jnp.zeros_like(los)], axis=1)
            adj = mm(jnp.concatenate([both, los], axis=0), mat, NT)
            adj = adj[:64] + adj[64:]
            adj = jnp.concatenate([adj[16 * q : 16 * q + 16] for q in range(4)], axis=1)
            return adj.astype(BF16)

        def project(adj, n):
            at = pl.multiple_of(n * GROUP * 512, GROUP * 512)
            return mm(adj, B[pl.ds(at, GROUP * 512), :], NN)

        def spreads(vals, n):
            return jnp.concatenate(
                [spread(vals[k], n * GROUP + k) for k in range(GROUP)], axis=1
            )

        def slot_rows(n):
            return tuple(slots(n * GROUP + k) for k in range(GROUP))

        last = 64 // GROUP - 1

        def back(n, carry):
            acc, adj, vals = carry
            acc = acc + project(adj, n)
            nxt = spreads(vals, n + 1)
            return acc, nxt, slot_rows(jnp.minimum(n + 2, last))

        start = (jnp.zeros((16, 256), F32), spreads(slot_rows(0), 0), slot_rows(1))
        acc, adj, _ = lax.fori_loop(0, last, back, start)
        acc = acc + project(adj, last)
        acc_out[t] = acc

        def send_sum(i, carry):
            pltpu.make_async_remote_copy(
                src_ref=acc_out.at[t],
                dst_ref=ar_in.at[t, g],
                send_sem=ar_send.at[t],
                recv_sem=ar_recv.at[t],
                device_id=(window_at(i), m),
                device_id_type=MESH,
            ).start()
            return carry

        lax.fori_loop(0, n_grid - 1, send_sum, 0)
        ar_in[t, g] = acc
        wait_bytes(ar_in.at[t, pl.ds(0, n_grid - 1)], ar_recv.at[t])
        total = ar_in[t, 0]
        for l in range(1, n_grid):
            total = total + ar_in[t, l]
        total = vec[...] + total
        vec[...] = total
        out[...] = total

    hessian(0, out1)
    hessian(1, out2)

    for t in range(2):
        wait_bytes(R.at[t, pl.ds(0, n_all - 1)], e1_send.at[t])
        wait_bytes(D.at[t, pl.ds(0, n_all - 1)], e2_send.at[t])
        wait_bytes(ar_in.at[t, pl.ds(0, n_grid - 1)], ar_send.at[t])


def local(
    pod_basis,
    probe_vectors,
    drifter_tiles,
    tile_counts,
    stencil_offsets,
    stencil_weights,
    error_scales,
    time_precision,
    *,
    n_grid,
    n_mode,
):
    vmem = pl.BlockSpec(memory_space=pltpu.VMEM)
    hbm = pl.BlockSpec(memory_space=pltpu.HBM)
    dma = pltpu.SemaphoreType.DMA
    table = pltpu.VMEM((64, 128), I32)
    n_all = n_grid * n_mode
    return pl.pallas_call(
        functools.partial(kernel, n_grid, n_mode),
        out_shape=(jax.ShapeDtypeStruct(probe_vectors.shape, F32),) * 2,
        in_specs=[hbm] * 8,
        out_specs=(vmem, vmem),
        scratch_shapes=[
            pltpu.VMEM(pod_basis.shape, BF16),
            pltpu.VMEM((64 * 128, 256), BF16),
            pltpu.VMEM((1, 4096), I32),
            pltpu.VMEM((1, 256), I32),
            pltpu.VMEM((4, 1, 4096), I32),
            pltpu.VMEM((4, 1, 4096), F32),
            pltpu.VMEM((1, 4096), F32),
            pltpu.SMEM((16, 16), F32),
            pltpu.VMEM((4, 64, 128), I32),
            pltpu.VMEM((4, 64, 128), F32),
            table,
            table,
            pltpu.VMEM((1, 4096), I32),
            pltpu.VMEM((1, 4096), F32),
            pltpu.VMEM((1, 4096), I32),
            pltpu.VMEM((128, 4096), BF16),
            pltpu.VMEM((1024, 128), F32),
            pltpu.VMEM((1024, 256), BF16),
            pltpu.VMEM((2, n_all, 4, 128), F32),
            pltpu.VMEM((2, n_all, 4, 128), F32),
            pltpu.VMEM((2, n_grid, 4, 128), F32),
            pltpu.VMEM((2, n_all, 4, 128), F32),
            pltpu.VMEM((512, 128), F32),
            pltpu.VMEM((2, 16, 256), F32),
            pltpu.VMEM((2, n_grid, 16, 256), F32),
            pltpu.VMEM((16, 256), F32),
            dma((LOADS,)),
            dma((7,)),
            dma((2,)),
            dma((2,)),
            dma((2,)),
            dma((2,)),
            dma((2,)),
            dma((2,)),
        ],
        compiler_params=pltpu.CompilerParams(
            collective_id=0, has_side_effects=True, vmem_limit_bytes=64 * 1024 * 1024
        ),
    )(
        pod_basis,
        probe_vectors,
        drifter_tiles,
        tile_counts.reshape(1, -1),
        stencil_offsets,
        stencil_weights,
        error_scales,
        time_precision,
    )


def solution(mesh):
    return jax.shard_map(
        functools.partial(local, n_grid=mesh.shape["grid"], n_mode=mesh.shape["mode"]),
        mesh=mesh,
        in_specs=(
            P("grid", "mode"),
            P(None, "mode"),
            P("grid", None),
            P("grid"),
            P(None, "grid", None),
            P(None, "grid", None),
            P("grid", None),
            P(),
        ),
        out_specs=(P(None, "mode"), P(None, "mode")),
        check_vma=False,
    )
```
